32 devices in a mesh: band: 8 (over z, x), seg: 4 (over y, core).
Axes of the slice: x: 2, y: 2, z: 4, core: 2. Of those that a mesh axis runs over, the one named last changes fastest.
Arguments:
- voltages: float32 [4, 1, 2, 2, 256, 3072], P('seg', None, None, None, 'band'), may hold values from -6 to 6
- chirp_phase: float32 [1, 256, 4096], P(None, 'seg', 'band'), may hold values from -3.140625 to 3.140625
Outputs:
- dedispersed: float32 [4, 1, 2, 2, 256, 3072], P('seg', None, None, None, 'band')
The draws below stay inside these ranges and needn't reach their ends.
All inputs are finite; a program needn't handle non-finite values.
Results may differ from the reference program's by a relative error of at most 0.00015.
Values sent between devices are 32-bit elements; how exact they have to be, the bound alone decides.
A program may use at most 64 MiB of HBM per device.

```python
import jax
import jax.numpy as jnp
from jax import lax

SUB = 1
COLS = 4096
ROWS = 256
VALID_COLS = 3072
LENGTH = 1048576
SEGS = 4


def steps_of(rng, extent, pieces, least, largest):
    gain = 1.0
    for position, blocks in pieces:
        steps = jax.random.uniform(jax.random.fold_in(jax.random.fold_in(rng, 6), position), (blocks,), jnp.float32, least / len(pieces), largest / len(pieces))
        gain = gain * jnp.repeat(jnp.exp(steps), extent[position] // blocks).reshape((-1,) + (1,) * (len(extent) - 1 - position))
    return gain


def scatter_about(rng, shape, width, bound, split=(), held_as=jnp.bfloat16):
    entries = jax.random.normal(rng, shape, jnp.float32) * width
    if len(split) > 0:
        entries = steps_of(rng, shape, split, -0.22, 0.18) * entries
    return jnp.clip(entries, min=-bound, max=bound).astype(held_as)


def setup_inputs(seed: int = 0) -> dict:
    splits = jax.random.split(jax.random.key(seed), 3)
    return {
        "voltages": scatter_about(splits[0], (SEGS, SUB, 2, 2, ROWS, VALID_COLS), 1.0, 6.0, ((0, 4), (4, 8)), jnp.float32),
        "chirp_phase": jnp.clip(jax.random.uniform(splits[1], (SUB, ROWS, COLS), jnp.float32, -3.140625, 3.140625), -3.140625, 3.140625),
    }


def reference(voltages, chirp_phase):
    lead_in = ROWS * COLS // 4
    valid = ROWS * VALID_COLS
    series = lax.complex(voltages[:, :, :, 0], voltages[:, :, :, 1])
    series = jnp.swapaxes(series, -1, -2).reshape(SEGS, SUB, 2, valid)
    series = jnp.moveaxis(series, 0, 2).reshape(SUB, 2, SEGS * valid)
    padded = jnp.concatenate([jnp.zeros((SUB, 2, lead_in), dtype=series.dtype), series], axis=-1)
    chirp = lax.complex(jnp.cos(chirp_phase), jnp.sin(chirp_phase)).reshape(SUB, 1, LENGTH)
    results = []
    for segment in range(SEGS):
        buffer = padded[:, :, segment * valid: segment * valid + LENGTH]
        spectrum = jnp.fft.fft(buffer, axis=-1) * chirp
        restored = jnp.fft.ifft(spectrum, axis=-1)[:, :, lead_in:]
        restored = jnp.swapaxes(restored.reshape(SUB, 2, VALID_COLS, ROWS), -1, -2)
        results.append(jnp.stack([jnp.real(restored), jnp.imag(restored)], axis=2))
    return jnp.stack(results, axis=0).astype(jnp.float32)
```

```python
import functools
import math

import jax
import jax.numpy as jnp
import numpy as np
from jax import lax
from jax.experimental import pallas as pl
from jax.experimental.pallas import tpu as pltpu
from jax.sharding import PartitionSpec as P

LANES = 128
SUBLANES = 8
VMEM_LIMIT = 56 * 1024 * 1024


def split_table(table):
    high = table.astype(jnp.bfloat16)
    low = (table - high.astype(np.float64)).astype(jnp.bfloat16)
    return high, low


def lane_table(direction):
    places = np.arange(LANES)
    angles = direction * 2.0 * np.pi / LANES * (places[:, None] * places[None, :] % LANES)
    cosine, sine = np.cos(angles), np.sin(angles)
    return split_table(np.block([[cosine, sine], [-sine, cosine]]))


def row_table(rows):
    places = np.arange(rows)
    angles = 2.0 * np.pi / rows * (places[:, None] * places[None, :] % rows)
    return split_table(np.concatenate([np.cos(angles), np.sin(angles)], axis=1))


def phase_table(product, length, direction, scale=1.0):
    angles = direction * 2.0 * np.pi / length * (product % length)
    return (np.stack([np.cos(angles), np.sin(angles)]) * scale).astype(np.float32)


def halves(value):
    high = value.astype(jnp.bfloat16)
    return high, (value - high.astype(jnp.float32)).astype(jnp.bfloat16)


def dot(left, right):
    return jnp.dot(left, right, preferred_element_type=jnp.float32)


def transform_list(pairs, direction):
    count = len(pairs)
    if count == 1:
        return pairs
    even = transform_list(pairs[0::2], direction)
    odd = transform_list(pairs[1::2], direction)
    first, second = [], []
    for k in range(count // 2):
        er, ei = even[k]
        pr, pi = odd[k]
        if k == 0:
            tr, ti = pr, pi
        elif 4 * k == count:
            tr, ti = (-pi, pr) if direction > 0 else (pi, -pr)
        else:
            c = math.cos(2.0 * math.pi * k / count)
            s = direction * math.sin(2.0 * math.pi * k / count)
            if 8 * k == count:
                tr, ti = (pr - direction * pi) * c, (pi + direction * pr) * c
            else:
                tr, ti = pr * c - pi * s, pr * s + pi * c
        first.append((er + tr, ei + ti))
        second.append((er - tr, ei - ti))
    return first + second


def forward_kernel(blocks, hist_ref, new_ref, inner_ref, outer_ref, high_ref, low_ref, out_ref):
    hist_blocks = hist_ref.shape[-1] // LANES
    pairs = []
    for j in range(blocks):
        if j < hist_blocks:
            cut = pl.ds(j * LANES, LANES)
            pairs.append((hist_ref[0, 0, 0, :, cut], hist_ref[0, 0, 1, :, cut]))
        else:
            cut = pl.ds((j - hist_blocks) * LANES, LANES)
            pairs.append((new_ref[0, 0, 0, 0, :, cut], new_ref[0, 0, 0, 1, :, cut]))
    lines = []
    for k, (real, imag) in enumerate(transform_list(pairs, -1.0)):
        cosine, sine = inner_ref[0, k : k + 1, :], inner_ref[1, k : k + 1, :]
        lines.append(
            jnp.concatenate([real * cosine - imag * sine, real * sine + imag * cosine], axis=1)
        )
    high, low = halves(jnp.concatenate(lines, axis=0))
    weights = high_ref[...]
    result = dot(high, weights) + dot(low, weights) + dot(high, low_ref[...])
    real, imag = result[:, :LANES], result[:, LANES:]
    cosine = outer_ref[0].reshape(real.shape)
    sine = outer_ref[1].reshape(real.shape)
    place = (out_ref.shape[0],) + out_ref.shape[2:]
    out_ref[:, 0] = (real * cosine - imag * sine).reshape(place)
    out_ref[:, 1] = (real * sine + imag * cosine).reshape(place)


def middle_kernel(in_ref, cos_ref, sin_ref, high_ref, low_ref, out_ref):
    bands, rows_dev = in_ref.shape[0], in_ref.shape[3]
    rows = bands * rows_dev
    high_table, low_table = high_ref[...], low_ref[...]

    def product(top, bottom):
        high, low = halves(jnp.concatenate([top, bottom], axis=0))
        return dot(high_table, high) + dot(high_table, low) + dot(low_table, high)

    real = in_ref[:, 0, 0].reshape(rows, LANES)
    imag = in_ref[:, 1, 0].reshape(rows, LANES)
    spectrum = product(
        jnp.concatenate([real, imag], axis=1), jnp.concatenate([imag, -real], axis=1)
    )
    real, imag = spectrum[:, :LANES], spectrum[:, LANES:]
    cosine, sine = cos_ref[0], sin_ref[0]
    real, imag = real * cosine - imag * sine, real * sine + imag * cosine
    restored = product(
        jnp.concatenate([real, imag], axis=1), jnp.concatenate([-imag, real], axis=1)
    )
    out_ref[:, 0, 0] = restored[:, :LANES].reshape(bands, rows_dev, LANES)
    out_ref[:, 1, 0] = restored[:, LANES:].reshape(bands, rows_dev, LANES)


def backward_kernel(blocks, in_ref, inner_ref, outer_ref, high_ref, low_ref, *rest):
    out_ref = rest[-1]
    lines = blocks * SUBLANES
    skipped = blocks - out_ref.shape[-1] // LANES
    real = in_ref[:, 0].reshape(lines, LANES)
    imag = in_ref[:, 1].reshape(lines, LANES)
    cosine = outer_ref[0].reshape(lines, LANES)
    sine = outer_ref[1].reshape(lines, LANES)
    high, low = halves(
        jnp.concatenate([real * cosine + imag * sine, imag * cosine - real * sine], axis=1)
    )
    weights = high_ref[...]
    result = dot(high, weights) + dot(low, weights) + dot(high, low_ref[...])
    pairs = []
    for k in range(blocks):
        cosine, sine = inner_ref[0, k : k + 1, :], inner_ref[1, k : k + 1, :]
        real = result[k * SUBLANES : (k + 1) * SUBLANES, :LANES]
        imag = result[k * SUBLANES : (k + 1) * SUBLANES, LANES:]
        pairs.append((real * cosine - imag * sine, real * sine + imag * cosine))
    restored = transform_list(pairs, 1.0)
    for j in range(skipped, blocks):
        cut = pl.ds((j - skipped) * LANES, LANES)
        out_ref[0, 0, 0, 0, :, cut] = restored[j][0]
        out_ref[0, 0, 0, 1, :, cut] = restored[j][1]


def whole(array):
    return pl.BlockSpec(array.shape, lambda i: (0,) * array.ndim)


def params():
    return pltpu.CompilerParams(vmem_limit_bytes=VMEM_LIMIT)


def per_device(voltages, chirp_phase):
    rows_dev, valid_cols = voltages.shape[4:]
    cols = valid_cols * 4 // 3
    bands = lax.axis_size("band")
    rows = rows_dev * bands
    length = rows * cols
    blocks = cols // LANES
    own_blocks = blocks // bands
    band = lax.axis_index("band")

    hist_cols = cols // 4
    tail = voltages[:, 0, :, :, :, valid_cols - hist_cols :]
    route = [(i - 1, i) for i in range(1, lax.axis_size("seg"))]
    history = lax.ppermute(tail, "seg", route)

    low_freq = np.arange(blocks)[:, None]
    freq = low_freq + blocks * np.arange(LANES)[None, :]
    inner_forward = jnp.asarray(phase_table(low_freq * np.arange(LANES)[None, :], cols, -1.0))
    inner_backward = jnp.asarray(
        phase_table(low_freq * np.arange(LANES)[None, :], cols, 1.0, 1.0 / length)
    )
    rest = jnp.asarray(
        phase_table(freq[:, None, :] * np.arange(rows_dev)[None, :, None], length, -1.0)
    )
    start = jnp.asarray(
        phase_table(freq[None] * (rows_dev * np.arange(bands))[:, None, None], length, -1.0)
    )
    start = lax.dynamic_index_in_dim(start, band, 1, keepdims=False)[:, :, None, :]
    outer = jnp.stack(
        [rest[0] * start[0] - rest[1] * start[1], rest[0] * start[1] + rest[1] * start[0]]
    )
    lane_forward = [jnp.asarray(t) for t in lane_table(-1.0)]
    lane_backward = [jnp.asarray(t) for t in lane_table(1.0)]
    row_tables = [jnp.asarray(t) for t in row_table(rows)]

    steps = rows_dev // SUBLANES
    sent_shape = (bands, 2, own_blocks, rows_dev, LANES)
    sent_spec = pl.BlockSpec(
        (bands, 2, own_blocks, SUBLANES, LANES), lambda i: (0, 0, 0, i, 0)
    )
    outer_spec = pl.BlockSpec((2, blocks, SUBLANES, LANES), lambda i: (0, 0, i, 0))

    def forward(pol):
        return pl.pallas_call(
            functools.partial(forward_kernel, blocks),
            grid=(steps,),
            in_specs=[
                pl.BlockSpec((1, 1, 2, SUBLANES, hist_cols), lambda i: (0, pol, 0, i, 0)),
                pl.BlockSpec(
                    (1, 1, 1, 2, SUBLANES, valid_cols), lambda i: (0, 0, pol, 0, i, 0)
                ),
                whole(inner_forward),
                outer_spec,
                whole(lane_forward[0]),
                whole(lane_forward[1]),
            ],
            out_specs=sent_spec,
            out_shape=jax.ShapeDtypeStruct(sent_shape, jnp.float32),
            compiler_params=params(),
            name="forward",
        )(history, voltages, inner_forward, outer, *lane_forward)

    def middle(received, cosine, sine):
        piece = pl.BlockSpec((bands, 2, 1, rows_dev, LANES), lambda i: (0, 0, i, 0, 0))
        phase = pl.BlockSpec((1, rows, LANES), lambda i: (i, 0, 0))
        return pl.pallas_call(
            middle_kernel,
            grid=(own_blocks,),
            in_specs=[piece, phase, phase, whole(row_tables[0]), whole(row_tables[1])],
            out_specs=piece,
            out_shape=jax.ShapeDtypeStruct(sent_shape, jnp.float32),
            compiler_params=params(),
            name="middle",
        )(received, cosine, sine, *row_tables)

    def backward(received, pol, into):
        extra = [] if into is None else [into]
        return pl.pallas_call(
            functools.partial(backward_kernel, blocks),
            grid=(steps,),
            in_specs=[
                sent_spec,
                whole(inner_backward),
                outer_spec,
                whole(lane_backward[0]),
                whole(lane_backward[1]),
            ]
            + [pl.BlockSpec(memory_space=pl.ANY)] * len(extra),
            out_specs=pl.BlockSpec(
                (1, 1, 1, 2, SUBLANES, valid_cols), lambda i: (0, 0, pol, 0, i, 0)
            ),
            out_shape=jax.ShapeDtypeStruct(voltages.shape, jnp.float32),
            input_output_aliases={5: 0} if extra else {},
            compiler_params=params(),
            name="backward",
        )(received, inner_backward, outer, *lane_backward, *extra)

    def exchange(block):
        return lax.all_to_all(block, "band", split_axis=0, concat_axis=0, tiled=True)

    seg_rows, width = chirp_phase.shape[1:]
    near = width // blocks
    phases = jnp.transpose(chirp_phase[0].reshape(seg_rows, near, blocks), (2, 0, 1))
    phases = exchange(phases.reshape(bands, own_blocks, seg_rows, near))
    phases = jnp.transpose(phases, (1, 2, 0, 3)).reshape(own_blocks, seg_rows, LANES)
    phases = lax.all_gather(phases, "seg", axis=1, tiled=True)
    cosine, sine = jnp.cos(phases), jnp.sin(phases)

    received = [exchange(forward(pol)) for pol in range(2)]
    returned = [exchange(middle(block, cosine, sine)) for block in received]
    result = None
    for pol in range(2):
        result = backward(returned[pol], pol, result)
    return result


def solution(mesh):
    in_specs = (P("seg", None, None, None, "band", None), P(None, "seg", "band"))
    out_specs = P("seg", None, None, None, "band", None)
    return jax.shard_map(
        per_device, mesh=mesh, in_specs=in_specs, out_specs=out_specs, check_vma=False
    )
```

```python
import functools
import math

import jax
import jax.numpy as jnp
import numpy as np
from jax import lax
from jax.experimental import pallas as pl
from jax.experimental.pallas import tpu as pltpu
from jax.sharding import PartitionSpec as P

LANES = 128
SUBLANES = 8
MESH = pl.DeviceIdType.MESH
VMEM_LIMIT = 56 * 1024 * 1024


def split_table(table):
    high = table.astype(jnp.bfloat16)
    low = (table - high.astype(np.float64)).astype(jnp.bfloat16)
    return high, low


def lane_table(direction):
    places = np.arange(LANES)
    angles = direction * 2.0 * np.pi / LANES * (places[:, None] * places[None, :] % LANES)
    cosine, sine = np.cos(angles), np.sin(angles)
    return split_table(np.block([[cosine, sine], [-sine, cosine]]))


def row_table(rows):
    places = np.arange(rows)
    angles = 2.0 * np.pi / rows * (places[:, None] * places[None, :] % rows)
    return split_table(np.concatenate([np.cos(angles), np.sin(angles)], axis=1))


def phase_table(product, length, direction, scale=1.0):
    angles = direction * 2.0 * np.pi / length * (product % length)
    return (np.stack([np.cos(angles), np.sin(angles)]) * scale).astype(np.float32)


def halves(value):
    high = value.astype(jnp.bfloat16)
    return high, (value - high.astype(jnp.float32)).astype(jnp.bfloat16)


def dot(left, right):
    return jnp.dot(left, right, preferred_element_type=jnp.float32)


def transform_list(pairs, direction):
    count = len(pairs)
    if count == 1:
        return pairs
    even = transform_list(pairs[0::2], direction)
    odd = transform_list(pairs[1::2], direction)
    first, second = [], []
    for k in range(count // 2):
        er, ei = even[k]
        pr, pi = odd[k]
        if k == 0:
            tr, ti = pr, pi
        elif 4 * k == count:
            tr, ti = (-pi, pr) if direction > 0 else (pi, -pr)
        else:
            c = math.cos(2.0 * math.pi * k / count)
            s = direction * math.sin(2.0 * math.pi * k / count)
            if 8 * k == count:
                tr, ti = (pr - direction * pi) * c, (pi + direction * pr) * c
            else:
                tr, ti = pr * c - pi * s, pr * s + pi * c
        first.append((er + tr, ei + ti))
        second.append((er - tr, ei - ti))
    return first + second


def split_dot(value, high_table, low_table):
    high, low = halves(value)
    return dot(high, high_table) + dot(low, high_table) + dot(high, low_table)


def forward_tile(blocks, pol, rows, hist_ref, new_ref, inner_ref, outer_ref, high_ref, low_ref, out_ref):
    hist_blocks = hist_ref.shape[-1] // LANES
    pairs = []
    for j in range(blocks):
        if j < hist_blocks:
            cut = pl.ds(j * LANES, LANES)
            pairs.append((hist_ref[0, pol, 0, rows, cut], hist_ref[0, pol, 1, rows, cut]))
        else:
            cut = pl.ds((j - hist_blocks) * LANES, LANES)
            pairs.append((new_ref[0, 0, pol, 0, rows, cut], new_ref[0, 0, pol, 1, rows, cut]))
    lines = []
    for k, (real, imag) in enumerate(transform_list(pairs, -1.0)):
        cosine, sine = inner_ref[0, k : k + 1, :], inner_ref[1, k : k + 1, :]
        lines.append(
            jnp.concatenate([real * cosine - imag * sine, real * sine + imag * cosine], axis=1)
        )
    result = split_dot(jnp.concatenate(lines, axis=0), high_ref[...], low_ref[...])
    real, imag = result[:, :LANES], result[:, LANES:]
    cosine = outer_ref[0, :, rows, :].reshape(real.shape)
    sine = outer_ref[1, :, rows, :].reshape(real.shape)
    bands, own = out_ref.shape[1], out_ref.shape[3]
    place = (bands, own, SUBLANES, LANES)
    out_ref[pol, :, 0, :, rows, :] = (real * cosine - imag * sine).reshape(place)
    out_ref[pol, :, 1, :, rows, :] = (real * sine + imag * cosine).reshape(place)


def middle_block(pol, block, in_ref, cos_ref, sin_ref, high_ref, low_ref, out_ref):
    bands, rows_dev = in_ref.shape[1], in_ref.shape[4]
    rows = bands * rows_dev
    high_table, low_table = high_ref[...], low_ref[...]

    def product(top, bottom):
        high, low = halves(jnp.concatenate([top, bottom], axis=0))
        return dot(high_table, high) + dot(high_table, low) + dot(low_table, high)

    real = in_ref[pol, :, 0, block].reshape(rows, LANES)
    imag = in_ref[pol, :, 1, block].reshape(rows, LANES)
    spectrum = product(
        jnp.concatenate([real, imag], axis=1), jnp.concatenate([imag, -real], axis=1)
    )
    real, imag = spectrum[:, :LANES], spectrum[:, LANES:]
    cosine, sine = cos_ref[block], sin_ref[block]
    real, imag = real * cosine - imag * sine, real * sine + imag * cosine
    restored = product(
        jnp.concatenate([real, imag], axis=1), jnp.concatenate([-imag, real], axis=1)
    )
    out_ref[pol, :, 0, block] = restored[:, :LANES].reshape(bands, rows_dev, LANES)
    out_ref[pol, :, 1, block] = restored[:, LANES:].reshape(bands, rows_dev, LANES)


def backward_tile(blocks, pol, rows, in_ref, inner_ref, outer_ref, high_ref, low_ref, out_ref):
    lines = blocks * SUBLANES
    skipped = blocks - out_ref.shape[-1] // LANES
    real = in_ref[pol, :, 0, :, rows, :].reshape(lines, LANES)
    imag = in_ref[pol, :, 1, :, rows, :].reshape(lines, LANES)
    cosine = outer_ref[0, :, rows, :].reshape(lines, LANES)
    sine = outer_ref[1, :, rows, :].reshape(lines, LANES)
    result = split_dot(
        jnp.concatenate([real * cosine + imag * sine, imag * cosine - real * sine], axis=1),
        high_ref[...],
        low_ref[...],
    )
    pairs = []
    for k in range(blocks):
        cosine, sine = inner_ref[0, k : k + 1, :], inner_ref[1, k : k + 1, :]
        real = result[k * SUBLANES : (k + 1) * SUBLANES, :LANES]
        imag = result[k * SUBLANES : (k + 1) * SUBLANES, LANES:]
        pairs.append((real * cosine - imag * sine, real * sine + imag * cosine))
    restored = transform_list(pairs, 1.0)
    for j in range(skipped, blocks):
        cut = pl.ds((j - skipped) * LANES, LANES)
        out_ref[0, 0, pol, 0, rows, cut] = restored[j][0]
        out_ref[0, 0, pol, 1, rows, cut] = restored[j][1]


def kernel(
    blocks,
    bands,
    segs,
    hist_ref,
    new_ref,
    phase_ref,
    inner_forward_ref,
    inner_backward_ref,
    outer_ref,
    forward_high,
    forward_low,
    backward_high,
    backward_low,
    row_high,
    row_low,
    out_ref,
    spread,
    received,
    restored,
    returned,
    gathered,
    cosines,
    sines,
    data_send,
    data_recv,
    phase_send,
    phase_recv,
):
    band, seg = lax.axis_index("band"), lax.axis_index("seg")
    own_blocks = spread.shape[3]
    rows_dev = spread.shape[4]
    rows = bands * rows_dev
    steps = rows_dev // SUBLANES

    barrier = pltpu.get_barrier_semaphore()
    for d in range(1, bands):
        pl.semaphore_signal(
            barrier, inc=1, device_id={"band": lax.rem(band + d, bands)}, device_id_type=MESH
        )
    for d in range(1, segs):
        pl.semaphore_signal(
            barrier, inc=1, device_id={"seg": lax.rem(seg + d, segs)}, device_id_type=MESH
        )
    pl.semaphore_wait(barrier, bands - 1 + segs - 1)

    def phase_copy(d):
        return pltpu.make_async_remote_copy(
            src_ref=phase_ref,
            dst_ref=gathered.at[seg],
            send_sem=phase_send.at[d],
            recv_sem=phase_recv.at[d],
            device_id={"seg": lax.rem(seg + d, segs)},
            device_id_type=MESH,
        )

    def data_copy(stage, pol, d):
        source, target = ((spread, received), (restored, returned))[stage]
        other = lax.rem(band + d, bands)
        return pltpu.make_async_remote_copy(
            src_ref=source.at[pol, other],
            dst_ref=target.at[pol, band],
            send_sem=data_send.at[stage, pol, d],
            recv_sem=data_recv.at[stage, pol, d],
            device_id={"band": other},
            device_id_type=MESH,
        )

    def send(stage, pol):
        for d in range(1, bands):
            data_copy(stage, pol, d).start()
        source, target = ((spread, received), (restored, returned))[stage]
        target[pol, band] = source[pol, band]

    def arrive(stage, pol):
        for d in range(1, bands):
            data_copy(stage, pol, d).wait_recv()

    for d in range(1, segs):
        phase_copy(d).start()
    gathered[seg] = phase_ref[...]

    def tile(i):
        return pl.ds(pl.multiple_of(i * SUBLANES, SUBLANES), SUBLANES)

    for pol in range(2):

        @pl.loop(0, steps)
        def _(i):
            forward_tile(
                blocks, pol, tile(i), hist_ref, new_ref, inner_forward_ref, outer_ref,
                forward_high, forward_low, spread,
            )

        send(0, pol)

    for d in range(1, segs):
        phase_copy(d).wait_recv()

    @pl.loop(0, own_blocks)
    def _(block):
        phases = gathered[:, block].reshape(rows, LANES)
        cosines[block] = jnp.cos(phases)
        sines[block] = jnp.sin(phases)

    for pol in range(2):
        arrive(0, pol)

        @pl.loop(0, own_blocks)
        def _(block):
            middle_block(pol, block, received, cosines, sines, row_high, row_low, restored)

        send(1, pol)

    for pol in range(2):
        arrive(1, pol)

        @pl.loop(0, steps)
        def _(i):
            backward_tile(
                blocks, pol, tile(i), returned, inner_backward_ref, outer_ref,
                backward_high, backward_low, out_ref,
            )

    for d in range(1, segs):
        phase_copy(d).wait_send()
    for stage in range(2):
        for pol in range(2):
            for d in range(1, bands):
                data_copy(stage, pol, d).wait_send()


def per_device(voltages, chirp_phase):
    rows_dev, valid_cols = voltages.shape[4:]
    cols = valid_cols * 4 // 3
    bands = lax.axis_size("band")
    rows = rows_dev * bands
    length = rows * cols
    blocks = cols // LANES
    own_blocks = blocks // bands
    band = lax.axis_index("band")

    hist_cols = cols // 4
    tail = voltages[:, 0, :, :, :, valid_cols - hist_cols :]
    route = [(i - 1, i) for i in range(1, lax.axis_size("seg"))]
    history = lax.ppermute(tail, "seg", route)

    low_freq = np.arange(blocks)[:, None]
    freq = low_freq + blocks * np.arange(LANES)[None, :]
    inner_forward = jnp.asarray(phase_table(low_freq * np.arange(LANES)[None, :], cols, -1.0))
    inner_backward = jnp.asarray(
        phase_table(low_freq * np.arange(LANES)[None, :], cols, 1.0, 1.0 / length)
    )
    rest = jnp.asarray(
        phase_table(freq[:, None, :] * np.arange(rows_dev)[None, :, None], length, -1.0)
    )
    start = jnp.asarray(
        phase_table(freq[None] * (rows_dev * np.arange(bands))[:, None, None], length, -1.0)
    )
    start = lax.dynamic_index_in_dim(start, band, 1, keepdims=False)[:, :, None, :]
    outer = jnp.stack(
        [rest[0] * start[0] - rest[1] * start[1], rest[0] * start[1] + rest[1] * start[0]]
    )
    lane_forward = [jnp.asarray(t) for t in lane_table(-1.0)]
    lane_backward = [jnp.asarray(t) for t in lane_table(1.0)]
    row_tables = [jnp.asarray(t) for t in row_table(rows)]

    seg_rows, width = chirp_phase.shape[1:]
    near = width // blocks
    phases = jnp.transpose(chirp_phase[0].reshape(seg_rows, near, blocks), (2, 0, 1))
    phases = lax.all_to_all(
        phases.reshape(bands, own_blocks, seg_rows, near),
        "band", split_axis=0, concat_axis=0, tiled=True,
    )
    phases = jnp.transpose(phases, (1, 2, 0, 3)).reshape(own_blocks, seg_rows, LANES)

    segs = lax.axis_size("seg")
    exchanged = pltpu.VMEM((2, bands, 2, own_blocks, rows_dev, LANES), jnp.float32)
    phase_space = pltpu.VMEM((own_blocks, rows, LANES), jnp.float32)
    operands = (
        history, voltages, phases, inner_forward, inner_backward, outer,
        *lane_forward, *lane_backward, *row_tables,
    )
    return pl.pallas_call(
        functools.partial(kernel, blocks, bands, segs),
        in_specs=[pl.BlockSpec(memory_space=pltpu.VMEM)] * len(operands),
        out_specs=pl.BlockSpec(memory_space=pltpu.VMEM),
        out_shape=jax.ShapeDtypeStruct(voltages.shape, jnp.float32),
        scratch_shapes=[exchanged] * 4
        + [
            pltpu.VMEM((segs, own_blocks, seg_rows, LANES), jnp.float32),
            phase_space,
            phase_space,
            pltpu.SemaphoreType.DMA((2, 2, bands)),
            pltpu.SemaphoreType.DMA((2, 2, bands)),
            pltpu.SemaphoreType.DMA((segs,)),
            pltpu.SemaphoreType.DMA((segs,)),
        ],
        compiler_params=pltpu.CompilerParams(
            vmem_limit_bytes=VMEM_LIMIT, collective_id=0, has_side_effects=True
        ),
        name="dedisperse",
    )(*operands)


def solution(mesh):
    in_specs = (P("seg", None, None, None, "band", None), P(None, "seg", "band"))
    out_specs = P("seg", None, None, None, "band", None)
    return jax.shard_map(
        per_device, mesh=mesh, in_specs=in_specs, out_specs=out_specs, check_vma=False
    )
```

```python
import functools
import math

import jax
import jax.numpy as jnp
import numpy as np
from jax import lax
from jax.experimental import pallas as pl
from jax.experimental.pallas import tpu as pltpu
from jax.sharding import PartitionSpec as P

LANES = 128
SUBLANES = 8
MESH = pl.DeviceIdType.MESH
VMEM_LIMIT = 56 * 1024 * 1024


def split_table(table):
    high = table.astype(jnp.bfloat16)
    low = (table - high.astype(np.float64)).astype(jnp.bfloat16)
    return high, low


def lane_table(direction):
    places = np.arange(LANES)
    angles = direction * 2.0 * np.pi / LANES * (places[:, None] * places[None, :] % LANES)
    cosine, sine = np.cos(angles), np.sin(angles)
    return split_table(np.block([[cosine, sine], [-sine, cosine]]))


def row_table(rows):
    places = np.arange(rows)
    angles = 2.0 * np.pi / rows * (places[:, None] * places[None, :] % rows)
    return split_table(np.concatenate([np.cos(angles), np.sin(angles)], axis=1))


def phase_table(product, length, direction, scale=1.0):
    angles = direction * 2.0 * np.pi / length * (product % length)
    return (np.stack([np.cos(angles), np.sin(angles)]) * scale).astype(np.float32)


def halves(value):
    high = value.astype(jnp.bfloat16)
    return high, (value - high.astype(jnp.float32)).astype(jnp.bfloat16)


def dot(left, right):
    return jnp.dot(left, right, preferred_element_type=jnp.float32)


def transform_list(pairs, direction):
    count = len(pairs)
    if count == 1:
        return pairs
    even = transform_list(pairs[0::2], direction)
    odd = transform_list(pairs[1::2], direction)
    first, second = [], []
    for k in range(count // 2):
        er, ei = even[k]
        pr, pi = odd[k]
        if k == 0:
            tr, ti = pr, pi
        elif 4 * k == count:
            tr, ti = (-pi, pr) if direction > 0 else (pi, -pr)
        else:
            c = math.cos(2.0 * math.pi * k / count)
            s = direction * math.sin(2.0 * math.pi * k / count)
            if 8 * k == count:
                tr, ti = (pr - direction * pi) * c, (pi + direction * pr) * c
            else:
                tr, ti = pr * c - pi * s, pr * s + pi * c
        first.append((er + tr, ei + ti))
        second.append((er - tr, ei - ti))
    return first + second


def split_dot(value, high_table, low_table):
    high, low = halves(value)
    return dot(high, high_table) + dot(low, high_table) + dot(high, low_table)


def forward_tile(blocks, pol, rows, hist_ref, new_ref, inner_ref, outer_ref, high_ref, low_ref, out_ref):
    hist_blocks = hist_ref.shape[-1] // LANES
    pairs = []
    for j in range(blocks):
        if j < hist_blocks:
            cut = pl.ds(j * LANES, LANES)
            pairs.append((hist_ref[0, pol, 0, rows, cut], hist_ref[0, pol, 1, rows, cut]))
        else:
            cut = pl.ds((j - hist_blocks) * LANES, LANES)
            pairs.append((new_ref[0, 0, pol, 0, rows, cut], new_ref[0, 0, pol, 1, rows, cut]))
    lines = []
    for k, (real, imag) in enumerate(transform_list(pairs, -1.0)):
        cosine, sine = inner_ref[0, k : k + 1, :], inner_ref[1, k : k + 1, :]
        lines.append(
            jnp.concatenate([real * cosine - imag * sine, real * sine + imag * cosine], axis=1)
        )
    result = split_dot(jnp.concatenate(lines, axis=0), high_ref[...], low_ref[...])
    real, imag = result[:, :LANES], result[:, LANES:]
    cosine = outer_ref[0, :, rows, :].reshape(real.shape)
    sine = outer_ref[1, :, rows, :].reshape(real.shape)
    bands, own = out_ref.shape[1], out_ref.shape[3]
    place = (bands, own, SUBLANES, LANES)
    out_ref[pol, :, 0, :, rows, :] = (real * cosine - imag * sine).reshape(place)
    out_ref[pol, :, 1, :, rows, :] = (real * sine + imag * cosine).reshape(place)


def middle_block(pol, block, in_ref, cos_ref, sin_ref, high_ref, low_ref, out_ref):
    bands, rows_dev = in_ref.shape[1], in_ref.shape[4]
    rows = bands * rows_dev
    high_table, low_table = high_ref[...], low_ref[...]

    def product(top, bottom):
        high, low = halves(jnp.concatenate([top, bottom], axis=0))
        return dot(high_table, high) + dot(high_table, low) + dot(low_table, high)

    real = in_ref[pol, :, 0, block].reshape(rows, LANES)
    imag = in_ref[pol, :, 1, block].reshape(rows, LANES)
    spectrum = product(
        jnp.concatenate([real, imag], axis=1), jnp.concatenate([imag, -real], axis=1)
    )
    real, imag = spectrum[:, :LANES], spectrum[:, LANES:]
    cosine, sine = cos_ref[block], sin_ref[block]
    real, imag = real * cosine - imag * sine, real * sine + imag * cosine
    restored = product(
        jnp.concatenate([real, imag], axis=1), jnp.concatenate([-imag, real], axis=1)
    )
    out_ref[pol, :, 0, block] = restored[:, :LANES].reshape(bands, rows_dev, LANES)
    out_ref[pol, :, 1, block] = restored[:, LANES:].reshape(bands, rows_dev, LANES)


def backward_tile(blocks, pol, rows, in_ref, inner_ref, outer_ref, high_ref, low_ref, out_ref):
    lines = blocks * SUBLANES
    skipped = blocks - out_ref.shape[-1] // LANES
    real = in_ref[pol, :, 0, :, rows, :].reshape(lines, LANES)
    imag = in_ref[pol, :, 1, :, rows, :].reshape(lines, LANES)
    cosine = outer_ref[0, :, rows, :].reshape(lines, LANES)
    sine = outer_ref[1, :, rows, :].reshape(lines, LANES)
    result = split_dot(
        jnp.concatenate([real * cosine + imag * sine, imag * cosine - real * sine], axis=1),
        high_ref[...],
        low_ref[...],
    )
    pairs = []
    for k in range(blocks):
        cosine, sine = inner_ref[0, k : k + 1, :], inner_ref[1, k : k + 1, :]
        real = result[k * SUBLANES : (k + 1) * SUBLANES, :LANES]
        imag = result[k * SUBLANES : (k + 1) * SUBLANES, LANES:]
        pairs.append((real * cosine - imag * sine, real * sine + imag * cosine))
    restored = transform_list(pairs, 1.0)
    for j in range(skipped, blocks):
        cut = pl.ds((j - skipped) * LANES, LANES)
        out_ref[0, 0, pol, 0, rows, cut] = restored[j][0]
        out_ref[0, 0, pol, 1, rows, cut] = restored[j][1]


def kernel(
    blocks,
    bands,
    segs,
    new_ref,
    chirp_ref,
    inner_forward_ref,
    inner_backward_ref,
    outer_ref,
    forward_high,
    forward_low,
    backward_high,
    backward_low,
    row_high,
    row_low,
    out_ref,
    spread,
    received,
    restored,
    returned,
    hist_ref,
    chirps,
    turned,
    gathered,
    cosines,
    sines,
    data_send,
    data_recv,
    phase_send,
    phase_recv,
    chirp_send,
    chirp_recv,
    hist_send,
    hist_recv,
):
    band, seg = lax.axis_index("band"), lax.axis_index("seg")
    own_blocks = spread.shape[3]
    rows_dev = spread.shape[4]
    rows = bands * rows_dev
    steps = rows_dev // SUBLANES

    barrier = pltpu.get_barrier_semaphore()
    for d in range(1, bands):
        pl.semaphore_signal(
            barrier, inc=1, device_id={"band": lax.rem(band + d, bands)}, device_id_type=MESH
        )
    for d in range(1, segs):
        pl.semaphore_signal(
            barrier, inc=1, device_id={"seg": lax.rem(seg + d, segs)}, device_id_type=MESH
        )
    pl.semaphore_wait(barrier, bands - 1 + segs - 1)

    def phase_copy(d):
        return pltpu.make_async_remote_copy(
            src_ref=gathered.at[seg],
            dst_ref=gathered.at[seg],
            send_sem=phase_send.at[d],
            recv_sem=phase_recv.at[d],
            device_id={"seg": lax.rem(seg + d, segs)},
            device_id_type=MESH,
        )

    def data_copy(stage, pol, d):
        source, target = ((spread, received), (restored, returned))[stage]
        other = lax.rem(band + d, bands)
        return pltpu.make_async_remote_copy(
            src_ref=source.at[pol, other],
            dst_ref=target.at[pol, band],
            send_sem=data_send.at[stage, pol, d],
            recv_sem=data_recv.at[stage, pol, d],
            device_id={"band": other},
            device_id_type=MESH,
        )

    def send(stage, pol):
        for d in range(1, bands):
            data_copy(stage, pol, d).start()
        source, target = ((spread, received), (restored, returned))[stage]
        target[pol, band] = source[pol, band]

    def arrive(stage, pol):
        for d in range(1, bands):
            data_copy(stage, pol, d).wait_recv()

    hist_cols = hist_ref.shape[-1]
    near = chirp_ref.shape[1] // own_blocks

    def hist_copy(pol):
        recent = pl.ds(new_ref.shape[-1] - hist_cols, hist_cols)
        return pltpu.make_async_remote_copy(
            src_ref=new_ref.at[0, 0, pol, :, :, recent],
            dst_ref=hist_ref.at[0, pol],
            send_sem=hist_send.at[pol],
            recv_sem=hist_recv.at[pol],
            device_id={"seg": lax.rem(seg + 1, segs)},
            device_id_type=MESH,
        )

    def chirp_copy(d):
        other = lax.rem(band + d, bands)
        return pltpu.make_async_remote_copy(
            src_ref=chirp_ref.at[other],
            dst_ref=chirps.at[band],
            send_sem=chirp_send.at[d],
            recv_sem=chirp_recv.at[d],
            device_id={"band": other},
            device_id_type=MESH,
        )

    @pl.when(seg < segs - 1)
    def _():
        for pol in range(2):
            hist_copy(pol).start()

    for d in range(1, bands):
        chirp_copy(d).start()
    chirps[band] = chirp_ref[band]

    @pl.when(seg == 0)
    def _():
        hist_ref[...] = jnp.zeros_like(hist_ref)

    def tile(i):
        return pl.ds(pl.multiple_of(i * SUBLANES, SUBLANES), SUBLANES)

    for pol in range(2):

        @pl.when(seg > 0)
        def _():
            hist_copy(pol).wait_recv()

        @pl.loop(0, steps)
        def _(i):
            forward_tile(
                blocks, pol, tile(i), hist_ref, new_ref, inner_forward_ref, outer_ref,
                forward_high, forward_low, spread,
            )

        send(0, pol)

    for d in range(1, bands):
        chirp_copy(d).wait_recv()
    for block in range(own_blocks):
        for source in range(bands):
            turned[block, source * near : (source + 1) * near] = chirps[
                source, block * near : (block + 1) * near
            ]
        gathered[seg, block] = jnp.transpose(turned[block])
    for d in range(1, segs):
        phase_copy(d).start()
    for d in range(1, segs):
        phase_copy(d).wait_recv()

    @pl.loop(0, own_blocks)
    def _(block):
        phases = gathered[:, block].reshape(rows, LANES)
        cosines[block] = jnp.cos(phases)
        sines[block] = jnp.sin(phases)

    for pol in range(2):
        arrive(0, pol)

        @pl.loop(0, own_blocks)
        def _(block):
            middle_block(pol, block, received, cosines, sines, row_high, row_low, restored)

        send(1, pol)

    for pol in range(2):
        arrive(1, pol)

        @pl.loop(0, steps)
        def _(i):
            backward_tile(
                blocks, pol, tile(i), returned, inner_backward_ref, outer_ref,
                backward_high, backward_low, out_ref,
            )

    @pl.when(seg < segs - 1)
    def _():
        for pol in range(2):
            hist_copy(pol).wait_send()

    for d in range(1, bands):
        chirp_copy(d).wait_send()
    for d in range(1, segs):
        phase_copy(d).wait_send()
    for stage in range(2):
        for pol in range(2):
            for d in range(1, bands):
                data_copy(stage, pol, d).wait_send()


def per_device(voltages, chirp_phase):
    rows_dev, valid_cols = voltages.shape[4:]
    cols = valid_cols * 4 // 3
    bands = lax.axis_size("band")
    rows = rows_dev * bands
    length = rows * cols
    blocks = cols // LANES
    own_blocks = blocks // bands
    band = lax.axis_index("band")

    hist_cols = cols // 4

    low_freq = np.arange(blocks)[:, None]
    freq = low_freq + blocks * np.arange(LANES)[None, :]
    inner_forward = jnp.asarray(phase_table(low_freq * np.arange(LANES)[None, :], cols, -1.0))
    inner_backward = jnp.asarray(
        phase_table(low_freq * np.arange(LANES)[None, :], cols, 1.0, 1.0 / length)
    )
    rest = jnp.asarray(
        phase_table(freq[:, None, :] * np.arange(rows_dev)[None, :, None], length, -1.0)
    )
    start = jnp.asarray(
        phase_table(freq[None] * (rows_dev * np.arange(bands))[:, None, None], length, -1.0)
    )
    start = lax.dynamic_index_in_dim(start, band, 1, keepdims=False)[:, :, None, :]
    outer = jnp.stack(
        [rest[0] * start[0] - rest[1] * start[1], rest[0] * start[1] + rest[1] * start[0]]
    )
    lane_forward = [jnp.asarray(t) for t in lane_table(-1.0)]
    lane_backward = [jnp.asarray(t) for t in lane_table(1.0)]
    row_tables = [jnp.asarray(t) for t in row_table(rows)]

    seg_rows, width = chirp_phase.shape[1:]
    near = width // blocks
    turned = jnp.transpose(chirp_phase[0]).reshape(near, blocks, seg_rows)
    turned = jnp.transpose(turned, (1, 0, 2)).reshape(bands, own_blocks * near, seg_rows)

    segs = lax.axis_size("seg")
    exchanged = pltpu.VMEM((2, bands, 2, own_blocks, rows_dev, LANES), jnp.float32)
    phase_space = pltpu.VMEM((own_blocks, rows, LANES), jnp.float32)
    operands = (
        voltages, turned, inner_forward, inner_backward, outer,
        *lane_forward, *lane_backward, *row_tables,
    )
    return pl.pallas_call(
        functools.partial(kernel, blocks, bands, segs),
        in_specs=[pl.BlockSpec(memory_space=pltpu.VMEM)] * len(operands),
        out_specs=pl.BlockSpec(memory_space=pltpu.VMEM),
        out_shape=jax.ShapeDtypeStruct(voltages.shape, jnp.float32),
        scratch_shapes=[exchanged] * 4
        + [
            pltpu.VMEM((1, 2, 2, rows_dev, hist_cols), jnp.float32),
            pltpu.VMEM((bands, own_blocks * near, seg_rows), jnp.float32),
            pltpu.VMEM((own_blocks, LANES, seg_rows), jnp.float32),
            pltpu.VMEM((segs, own_blocks, seg_rows, LANES), jnp.float32),
            phase_space,
            phase_space,
            pltpu.SemaphoreType.DMA((2, 2, bands)),
            pltpu.SemaphoreType.DMA((2, 2, bands)),
            pltpu.SemaphoreType.DMA((segs,)),
            pltpu.SemaphoreType.DMA((segs,)),
            pltpu.SemaphoreType.DMA((bands,)),
            pltpu.SemaphoreType.DMA((bands,)),
            pltpu.SemaphoreType.DMA((2,)),
            pltpu.SemaphoreType.DMA((2,)),
        ],
        compiler_params=pltpu.CompilerParams(
            vmem_limit_bytes=VMEM_LIMIT, collective_id=0, has_side_effects=True
        ),
        name="dedisperse",
    )(*operands)


def solution(mesh):
    in_specs = (P("seg", None, None, None, "band", None), P(None, "seg", "band"))
    out_specs = P("seg", None, None, None, "band", None)
    return jax.shard_map(
        per_device, mesh=mesh, in_specs=in_specs, out_specs=out_specs, check_vma=False
    )
```

```python
import functools
import math

import jax
import jax.numpy as jnp
import numpy as np
from jax import lax
from jax.experimental import pallas as pl
from jax.experimental.pallas import tpu as pltpu
from jax.sharding import PartitionSpec as P

LANES = 128
SUBLANES = 8
MESH = pl.DeviceIdType.MESH
VMEM_LIMIT = 56 * 1024 * 1024


def split_table(table):
    high = table.astype(jnp.bfloat16)
    low = (table - high.astype(np.float64)).astype(jnp.bfloat16)
    return high, low


def lane_table(direction):
    places = np.arange(LANES)
    angles = direction * 2.0 * np.pi / LANES * (places[:, None] * places[None, :] % LANES)
    cosine, sine = np.cos(angles), np.sin(angles)
    return split_table(np.block([[cosine, sine], [-sine, cosine]]))


def row_table(rows):
    places = np.arange(rows)
    angles = 2.0 * np.pi / rows * (places[:, None] * places[None, :] % rows)
    return split_table(np.concatenate([np.cos(angles), np.sin(angles)], axis=1))


def phase_table(product, length, direction, scale=1.0):
    angles = direction * 2.0 * np.pi / length * (product % length)
    return (np.stack([np.cos(angles), np.sin(angles)]) * scale).astype(np.float32)


def halves(value):
    high = value.astype(jnp.bfloat16)
    return high, (value - high.astype(jnp.float32)).astype(jnp.bfloat16)


def dot(left, right):
    return jnp.dot(left, right, preferred_element_type=jnp.float32)


def transform_list(pairs, direction):
    count = len(pairs)
    if count == 1:
        return pairs
    even = transform_list(pairs[0::2], direction)
    odd = transform_list(pairs[1::2], direction)
    first, second = [], []
    for k in range(count // 2):
        er, ei = even[k]
        pr, pi = odd[k]
        if k == 0:
            tr, ti = pr, pi
        elif 4 * k == count:
            tr, ti = (-pi, pr) if direction > 0 else (pi, -pr)
        else:
            c = math.cos(2.0 * math.pi * k / count)
            s = direction * math.sin(2.0 * math.pi * k / count)
            if 8 * k == count:
                tr, ti = (pr - direction * pi) * c, (pi + direction * pr) * c
            else:
                tr, ti = pr * c - pi * s, pr * s + pi * c
        first.append((er + tr, ei + ti))
        second.append((er - tr, ei - ti))
    return first + second


def split_dot(value, high_table, low_table):
    high, low = halves(value)
    return dot(high, high_table) + dot(low, high_table) + dot(high, low_table)


def forward_tile(blocks, pol, rows, hist_ref, new_ref, inner_ref, outer_ref, high_ref, low_ref, out_ref):
    hist_blocks = hist_ref.shape[-1] // LANES
    pairs = []
    for j in range(blocks):
        if j < hist_blocks:
            cut = pl.ds(j * LANES, LANES)
            pairs.append((hist_ref[0, pol, 0, rows, cut], hist_ref[0, pol, 1, rows, cut]))
        else:
            cut = pl.ds((j - hist_blocks) * LANES, LANES)
            pairs.append((new_ref[0, 0, pol, 0, rows, cut], new_ref[0, 0, pol, 1, rows, cut]))
    lines = []
    for k, (real, imag) in enumerate(transform_list(pairs, -1.0)):
        cosine, sine = inner_ref[0, k : k + 1, :], inner_ref[1, k : k + 1, :]
        lines.append(
            jnp.concatenate([real * cosine - imag * sine, real * sine + imag * cosine], axis=1)
        )
    result = split_dot(jnp.concatenate(lines, axis=0), high_ref[...], low_ref[...])
    real, imag = result[:, :LANES], result[:, LANES:]
    cosine = outer_ref[0, :, rows, :].reshape(real.shape)
    sine = outer_ref[1, :, rows, :].reshape(real.shape)
    bands, own = out_ref.shape[1], out_ref.shape[3]
    place = (bands, own, SUBLANES, LANES)
    out_ref[pol, :, 0, :, rows, :] = (real * cosine - imag * sine).reshape(place)
    out_ref[pol, :, 1, :, rows, :] = (real * sine + imag * cosine).reshape(place)


def middle_block(pol, block, in_ref, cos_ref, sin_ref, high_ref, low_ref, out_ref):
    bands, rows_dev = in_ref.shape[1], in_ref.shape[4]
    rows = bands * rows_dev
    high_table, low_table = high_ref[...], low_ref[...]

    def product(top, bottom):
        high, low = halves(jnp.concatenate([top, bottom], axis=0))
        return dot(high_table, high) + dot(high_table, low) + dot(low_table, high)

    real = in_ref[pol, :, 0, block].reshape(rows, LANES)
    imag = in_ref[pol, :, 1, block].reshape(rows, LANES)
    spectrum = product(
        jnp.concatenate([real, imag], axis=1), jnp.concatenate([imag, -real], axis=1)
    )
    real, imag = spectrum[:, :LANES], spectrum[:, LANES:]
    cosine, sine = cos_ref[block], sin_ref[block]
    real, imag = real * cosine - imag * sine, real * sine + imag * cosine
    restored = product(
        jnp.concatenate([real, imag], axis=1), jnp.concatenate([-imag, real], axis=1)
    )
    out_ref[pol, :, 0, block] = restored[:, :LANES].reshape(bands, rows_dev, LANES)
    out_ref[pol, :, 1, block] = restored[:, LANES:].reshape(bands, rows_dev, LANES)


def backward_tile(blocks, pol, rows, in_ref, inner_ref, outer_ref, high_ref, low_ref, out_ref):
    lines = blocks * SUBLANES
    skipped = blocks - out_ref.shape[-1] // LANES
    real = in_ref[pol, :, 0, :, rows, :].reshape(lines, LANES)
    imag = in_ref[pol, :, 1, :, rows, :].reshape(lines, LANES)
    cosine = outer_ref[0, :, rows, :].reshape(lines, LANES)
    sine = outer_ref[1, :, rows, :].reshape(lines, LANES)
    result = split_dot(
        jnp.concatenate([real * cosine + imag * sine, imag * cosine - real * sine], axis=1),
        high_ref[...],
        low_ref[...],
    )
    pairs = []
    for k in range(blocks):
        cosine, sine = inner_ref[0, k : k + 1, :], inner_ref[1, k : k + 1, :]
        real = result[k * SUBLANES : (k + 1) * SUBLANES, :LANES]
        imag = result[k * SUBLANES : (k + 1) * SUBLANES, LANES:]
        pairs.append((real * cosine - imag * sine, real * sine + imag * cosine))
    restored = transform_list(pairs, 1.0)
    for j in range(skipped, blocks):
        cut = pl.ds((j - skipped) * LANES, LANES)
        out_ref[0, 0, pol, 0, rows, cut] = restored[j][0]
        out_ref[0, 0, pol, 1, rows, cut] = restored[j][1]


def kernel(
    blocks,
    bands,
    segs,
    new_ref,
    chirp_ref,
    inner_forward_ref,
    inner_backward_ref,
    outer_ref,
    forward_high,
    forward_low,
    backward_high,
    backward_low,
    row_high,
    row_low,
    out_ref,
    spread,
    received,
    restored,
    returned,
    hist_ref,
    chirps,
    turned,
    gathered,
    cosines,
    sines,
    data_send,
    data_recv,
    phase_send,
    phase_recv,
    chirp_send,
    chirp_recv,
    hist_send,
    hist_recv,
):
    band, seg = lax.axis_index("band"), lax.axis_index("seg")
    own_blocks = spread.shape[3]
    rows_dev = spread.shape[4]
    rows = bands * rows_dev
    steps = rows_dev // SUBLANES

    barrier = pltpu.get_barrier_semaphore()
    for d in range(1, bands):
        pl.semaphore_signal(
            barrier, inc=1, device_id={"band": lax.rem(band + d, bands)}, device_id_type=MESH
        )
    for d in range(1, segs):
        pl.semaphore_signal(
            barrier, inc=1, device_id={"seg": lax.rem(seg + d, segs)}, device_id_type=MESH
        )
    pl.semaphore_wait(barrier, bands - 1 + segs - 1)

    def phase_copy(d):
        return pltpu.make_async_remote_copy(
            src_ref=gathered.at[seg],
            dst_ref=gathered.at[seg],
            send_sem=phase_send.at[d],
            recv_sem=phase_recv.at[d],
            device_id={"seg": lax.rem(seg + d, segs)},
            device_id_type=MESH,
        )

    def data_copy(stage, pol, half, d):
        part = pl.ds(half * (rows_dev // 2), rows_dev // 2)
        source, target = ((spread, received), (restored, returned))[stage]
        other = lax.rem(band + d, bands)
        return pltpu.make_async_remote_copy(
            src_ref=source.at[pol, other, :, :, part],
            dst_ref=target.at[pol, band, :, :, part],
            send_sem=data_send.at[stage, pol, half, d],
            recv_sem=data_recv.at[stage, pol, half, d],
            device_id={"band": other},
            device_id_type=MESH,
        )

    def send(stage, pol, half):
        for d in range(1, bands):
            data_copy(stage, pol, half, d).start()

    def keep(stage, pol):
        source, target = ((spread, received), (restored, returned))[stage]
        target[pol, band] = source[pol, band]

    def arrive(stage, pol, half):
        for d in range(1, bands):
            data_copy(stage, pol, half, d).wait_recv()

    hist_cols = hist_ref.shape[-1]
    near = chirp_ref.shape[1] // own_blocks

    def hist_copy(pol):
        recent = pl.ds(new_ref.shape[-1] - hist_cols, hist_cols)
        return pltpu.make_async_remote_copy(
            src_ref=new_ref.at[0, 0, pol, :, :, recent],
            dst_ref=hist_ref.at[0, pol],
            send_sem=hist_send.at[pol],
            recv_sem=hist_recv.at[pol],
            device_id={"seg": lax.rem(seg + 1, segs)},
            device_id_type=MESH,
        )

    def chirp_copy(d):
        other = lax.rem(band + d, bands)
        return pltpu.make_async_remote_copy(
            src_ref=chirp_ref.at[other],
            dst_ref=chirps.at[band],
            send_sem=chirp_send.at[d],
            recv_sem=chirp_recv.at[d],
            device_id={"band": other},
            device_id_type=MESH,
        )

    @pl.when(seg < segs - 1)
    def _():
        for pol in range(2):
            hist_copy(pol).start()

    for d in range(1, bands):
        chirp_copy(d).start()
    chirps[band] = chirp_ref[band]

    @pl.when(seg == 0)
    def _():
        hist_ref[...] = jnp.zeros_like(hist_ref)

    def tile(i):
        return pl.ds(pl.multiple_of(i * SUBLANES, SUBLANES), SUBLANES)

    for pol in range(2):

        @pl.when(seg > 0)
        def _():
            hist_copy(pol).wait_recv()

        for half in range(2):

            @pl.loop(half * (steps // 2), (half + 1) * (steps // 2))
            def _(i):
                forward_tile(
                    blocks, pol, tile(i), hist_ref, new_ref, inner_forward_ref, outer_ref,
                    forward_high, forward_low, spread,
                )

            send(0, pol, half)
        keep(0, pol)

    for d in range(1, bands):
        chirp_copy(d).wait_recv()
    for block in range(own_blocks):
        for source in range(bands):
            turned[block, source * near : (source + 1) * near] = chirps[
                source, block * near : (block + 1) * near
            ]
        gathered[seg, block] = jnp.transpose(turned[block])
    for d in range(1, segs):
        phase_copy(d).start()
    for d in range(1, segs):
        phase_copy(d).wait_recv()

    @pl.loop(0, own_blocks)
    def _(block):
        phases = gathered[:, block].reshape(rows, LANES)
        cosines[block] = jnp.cos(phases)
        sines[block] = jnp.sin(phases)

    for pol in range(2):
        for half in range(2):
            arrive(0, pol, half)

        @pl.loop(0, own_blocks)
        def _(block):
            middle_block(pol, block, received, cosines, sines, row_high, row_low, restored)

        for half in range(2):
            send(1, pol, half)
        keep(1, pol)

    for pol in range(2):
        for half in range(2):
            arrive(1, pol, half)

            @pl.loop(half * (steps // 2), (half + 1) * (steps // 2))
            def _(i):
                backward_tile(
                    blocks, pol, tile(i), returned, inner_backward_ref, outer_ref,
                    backward_high, backward_low, out_ref,
                )

    @pl.when(seg < segs - 1)
    def _():
        for pol in range(2):
            hist_copy(pol).wait_send()

    for d in range(1, bands):
        chirp_copy(d).wait_send()
    for d in range(1, segs):
        phase_copy(d).wait_send()
    for stage in range(2):
        for pol in range(2):
            for half in range(2):
                for d in range(1, bands):
                    data_copy(stage, pol, half, d).wait_send()


def per_device(voltages, chirp_phase):
    rows_dev, valid_cols = voltages.shape[4:]
    cols = valid_cols * 4 // 3
    bands = lax.axis_size("band")
    rows = rows_dev * bands
    length = rows * cols
    blocks = cols // LANES
    own_blocks = blocks // bands
    band = lax.axis_index("band")

    hist_cols = cols // 4

    low_freq = np.arange(blocks)[:, None]
    freq = low_freq + blocks * np.arange(LANES)[None, :]
    inner_forward = jnp.asarray(phase_table(low_freq * np.arange(LANES)[None, :], cols, -1.0))
    inner_backward = jnp.asarray(
        phase_table(low_freq * np.arange(LANES)[None, :], cols, 1.0, 1.0 / length)
    )
    rest = jnp.asarray(
        phase_table(freq[:, None, :] * np.arange(rows_dev)[None, :, None], length, -1.0)
    )
    start = jnp.asarray(
        phase_table(freq[None] * (rows_dev * np.arange(bands))[:, None, None], length, -1.0)
    )
    start = lax.dynamic_index_in_dim(start, band, 1, keepdims=False)[:, :, None, :]
    outer = jnp.stack(
        [rest[0] * start[0] - rest[1] * start[1], rest[0] * start[1] + rest[1] * start[0]]
    )
    lane_forward = [jnp.asarray(t) for t in lane_table(-1.0)]
    lane_backward = [jnp.asarray(t) for t in lane_table(1.0)]
    row_tables = [jnp.asarray(t) for t in row_table(rows)]

    seg_rows, width = chirp_phase.shape[1:]
    near = width // blocks
    turned = jnp.transpose(chirp_phase[0]).reshape(near, blocks, seg_rows)
    turned = jnp.transpose(turned, (1, 0, 2)).reshape(bands, own_blocks * near, seg_rows)

    segs = lax.axis_size("seg")
    exchanged = pltpu.VMEM((2, bands, 2, own_blocks, rows_dev, LANES), jnp.float32)
    phase_space = pltpu.VMEM((own_blocks, rows, LANES), jnp.float32)
    operands = (
        voltages, turned, inner_forward, inner_backward, outer,
        *lane_forward, *lane_backward, *row_tables,
    )
    return pl.pallas_call(
        functools.partial(kernel, blocks, bands, segs),
        in_specs=[pl.BlockSpec(memory_space=pltpu.VMEM)] * len(operands),
        out_specs=pl.BlockSpec(memory_space=pltpu.VMEM),
        out_shape=jax.ShapeDtypeStruct(voltages.shape, jnp.float32),
        scratch_shapes=[exchanged] * 4
        + [
            pltpu.VMEM((1, 2, 2, rows_dev, hist_cols), jnp.float32),
            pltpu.VMEM((bands, own_blocks * near, seg_rows), jnp.float32),
            pltpu.VMEM((own_blocks, LANES, seg_rows), jnp.float32),
            pltpu.VMEM((segs, own_blocks, seg_rows, LANES), jnp.float32),
            phase_space,
            phase_space,
            pltpu.SemaphoreType.DMA((2, 2, 2, bands)),
            pltpu.SemaphoreType.DMA((2, 2, 2, bands)),
            pltpu.SemaphoreType.DMA((segs,)),
            pltpu.SemaphoreType.DMA((segs,)),
            pltpu.SemaphoreType.DMA((bands,)),
            pltpu.SemaphoreType.DMA((bands,)),
            pltpu.SemaphoreType.DMA((2,)),
            pltpu.SemaphoreType.DMA((2,)),
        ],
        compiler_params=pltpu.CompilerParams(
            vmem_limit_bytes=VMEM_LIMIT, collective_id=0, has_side_effects=True
        ),
        name="dedisperse",
    )(*operands)


def solution(mesh):
    in_specs = (P("seg", None, None, None, "band", None), P(None, "seg", "band"))
    out_specs = P("seg", None, None, None, "band", None)
    return jax.shard_map(
        per_device, mesh=mesh, in_specs=in_specs, out_specs=out_specs, check_vma=False
    )
```
